32 devices in a mesh: gx: 4 (over z), gy: 8 (over y, x, core).
Axes of the slice: x: 2, y: 2, z: 4, core: 2. Of those that a mesh axis runs over, the one named last changes fastest.
Arguments:
- start_coeffs: float32 [9, 512, 2048], P(None, 'gy', 'gx'), may hold values from -6 to 6
- section_coeffs: float32 [9, 512, 2048], P(None, 'gy', 'gx'), may hold values from -6 to 6
- vel_x: float32 [512, 2048], P('gy', 'gx'), may hold values from -1 to 1
- vel_y: float32 [512, 2048], P('gy', 'gx'), may hold values from -1 to 1
Outputs:
- updated: float32 [9, 512, 2048], P(None, 'gy', 'gx')
- filtered: float32 [9, 512, 2048], P(None, 'gy', 'gx')
The draws below stay inside these ranges and needn't reach their ends.
All inputs are finite; a program needn't handle non-finite values.
Results may differ from the reference program's by a relative error of at most 0.0001.
Values sent between devices are 32-bit elements; how exact they have to be, the bound alone decides.
A program may use at most 64 MiB of HBM per device.

```python
import jax
import jax.numpy as jnp
import numpy as np
from jax import lax

MODES = 9
NX = 2048
NY = 512


def level_of(stream_key, extent, cuts, least, top_value):
    def one(axis_at, shards_of):
        draws = jax.random.uniform(jax.random.fold_in(jax.random.fold_in(stream_key, 6), axis_at), (shards_of,), jnp.float32, least / len(cuts), top_value / len(cuts))
        return jnp.repeat(jnp.exp(draws), extent[axis_at] // shards_of).reshape((-1,) + (1,) * (len(extent) - axis_at - 1))

    factor_of = one(*cuts[0])
    for cut in cuts[1:]:
        factor_of = factor_of * one(*cut)
    return factor_of


def bell_draw(key, extent, spread, most, cuts=(), held_as=jnp.bfloat16):
    values = spread * jax.random.normal(key, extent, jnp.float32)
    if cuts:
        values = values * level_of(key, extent, cuts, -0.22, 0.18)
    return jnp.clip(values, -most, most).astype(held_as)


def setup_inputs(seed: int = 0) -> dict:
    keys = jax.random.split(jax.random.key(seed), 5)
    start_coeffs = bell_draw(keys[0], (MODES, NY, NX), 1.0, 6.0, ((1, 8), (2, 4)), jnp.float32)
    section_coeffs = bell_draw(keys[1], (MODES, NY, NX), 1.0, 6.0, ((1, 8), (2, 4)), jnp.float32)
    vel_x = jnp.clip(jax.random.uniform(keys[2], (NY, NX), jnp.float32, -1.0, 1.0) * level_of(keys[2], (NY, NX), ((0, 8), (1, 4)), -0.4, 0.0), -1.0, 1.0)
    vel_y = jnp.clip(jax.random.uniform(keys[3], (NY, NX), jnp.float32, -1.0, 1.0) * level_of(keys[3], (NY, NX), ((0, 8), (1, 4)), -0.4, 0.0), -1.0, 1.0)
    return {"start_coeffs": start_coeffs, "section_coeffs": section_coeffs, "vel_x": vel_x, "vel_y": vel_y}


STEP_SIZE = 0.3
GAUSS_NODES = (-0.9324695142031521, -0.6612093864662645, -0.2386191860831969, 0.2386191860831969, 0.6612093864662645, 0.9324695142031521)
GAUSS_WEIGHTS = (0.1713244923791704, 0.3607615730481386, 0.4679139345726910, 0.4679139345726910, 0.3607615730481386, 0.1713244923791704)


def legendre_rows(points):
    return np.stack([points * 0.0 + 1.0, points, 1.5 * points * points - 0.5])


def bspline(points):
    magnitude = np.abs(points)
    return np.where(magnitude <= 0.5, 0.75 - magnitude * magnitude, np.where(magnitude <= 1.5, 0.5 * (1.5 - magnitude) ** 2, 0.0))


def kernel_value(points):
    return 1.25 * bspline(points) - 0.125 * (bspline(points + 1.0) + bspline(points - 1.0))


def siac_table():
    nodes = np.array(GAUSS_NODES)
    weights = np.array(GAUSS_WEIGHTS)
    kernel_table = np.zeros((5, 3, 3))
    for slot_index in range(5):
        offset = slot_index - 2
        for low_end, high_end in ((-1.0, 0.0), (0.0, 1.0)):
            for node_value, node_weight in zip(GAUSS_NODES, GAUSS_WEIGHTS):
                xi_value = 0.5 * (low_end + high_end) + 0.5 * (high_end - low_end) * node_value
                outer_weight = 0.5 * (high_end - low_end) * node_weight
                breaks = [-1.0, 1.0]
                for spline_knot in (-2.5, -1.5, -0.5, 0.5, 1.5, 2.5):
                    crossing = xi_value - 2.0 * offset - 2.0 * spline_knot
                    if -1.0 < crossing < 1.0:
                        breaks.append(crossing)
                breaks = sorted(breaks)
                for piece_lo, piece_hi in zip(breaks[:-1], breaks[1:]):
                    eta_points = 0.5 * (piece_lo + piece_hi) + 0.5 * (piece_hi - piece_lo) * nodes
                    eta_weights = 0.5 * (piece_hi - piece_lo) * weights
                    samples = kernel_value(0.5 * xi_value - 0.5 * eta_points - offset) * eta_weights * 0.5
                    kernel_table[slot_index] += outer_weight * np.outer(legendre_rows(np.array(xi_value)), legendre_rows(eta_points) @ samples)
    return kernel_table * (np.arange(3)[None, :, None] + 0.5)


def x_faces(coeffs):
    east_side = coeffs[0] + coeffs[1] + coeffs[2]
    west_side = coeffs[0] - coeffs[1] + coeffs[2]
    return east_side, west_side


def y_faces(coeffs):
    north_side = coeffs[:, 0] + coeffs[:, 1] + coeffs[:, 2]
    south_side = coeffs[:, 0] - coeffs[:, 1] + coeffs[:, 2]
    return north_side, south_side


def face_flux(inner, outer, speed_in, speed_out):
    speed = 0.5 * (speed_in + speed_out)
    return speed * (0.5 * (inner + outer)) - (0.5 * jnp.abs(speed)) * (outer - inner)


def tendency(coeffs, vel_x, vel_y, west, east, south, north):
    parity = (1.0, -1.0, 1.0)
    terms = []
    for deg_x in range(3):
        for deg_y in range(3):
            along_x = -(east[deg_y] - parity[deg_x] * west[deg_y])
            if deg_x > 0:
                along_x = 2.0 * vel_x * coeffs[deg_x - 1, deg_y] + along_x
            along_y = -(north[deg_x] - parity[deg_y] * south[deg_x])
            if deg_y > 0:
                along_y = 2.0 * vel_y * coeffs[deg_x, deg_y - 1] + along_y
            terms.append((deg_x + 0.5) * along_x + (deg_y + 0.5) * along_y)
    return jnp.stack(terms)


def advance(start_coeffs, section_coeffs, rate):
    return start_coeffs / 3.0 + (2.0 / 3.0) * (section_coeffs + STEP_SIZE * rate)


def reference(start_coeffs, section_coeffs, vel_x, vel_y):
    coeffs = section_coeffs.reshape(3, 3, NY, NX)
    east_x, west_x = x_faces(coeffs)
    east = face_flux(east_x, jnp.roll(west_x, -1, axis=-1), vel_x, jnp.roll(vel_x, -1, axis=-1))
    west = jnp.roll(east, 1, axis=-1)
    north_y, south_y = y_faces(coeffs)
    north = face_flux(north_y, jnp.roll(south_y, -1, axis=-2), vel_y, jnp.roll(vel_y, -1, axis=-2))
    south = jnp.roll(north, 1, axis=-2)
    rate = tendency(coeffs, vel_x, vel_y, west, east, south, north)
    updated = advance(start_coeffs, section_coeffs, rate)
    kernel_table = jnp.asarray(siac_table(), dtype=jnp.float32)
    grid = updated.reshape(3, 3, NY, NX)
    swept = None
    for slot in range(5):
        piece = jnp.roll(grid, 2 - slot, axis=-1)
        term = jnp.einsum('ac,cbyx->abyx', kernel_table[slot], piece, precision=lax.Precision.HIGHEST)
        swept = term if swept is None else swept + term
    filtered = None
    for slot in range(5):
        piece = jnp.roll(swept, 2 - slot, axis=-2)
        term = jnp.einsum('bd,adyx->abyx', kernel_table[slot], piece, precision=lax.Precision.HIGHEST)
        filtered = term if filtered is None else filtered + term
    return updated, filtered.reshape(9, NY, NX)
```

```python
import functools

import jax
import jax.numpy as jnp
import numpy as np
from jax import lax
from jax.experimental import pallas as pl
from jax.experimental.pallas import tpu as pltpu
from jax.sharding import PartitionSpec as P

STEP_SIZE = 0.3
GAUSS_NODES = (
    -0.932469514203152,
    -0.6612093864662645,
    -0.2386191860831969,
    0.2386191860831969,
    0.6612093864662645,
    0.932469514203152,
)
GAUSS_WEIGHTS = (
    0.1713244923791704,
    0.3607615730481386,
    0.467913934572691,
    0.467913934572691,
    0.3607615730481386,
    0.1713244923791704,
)


def legendre_rows(points):
    return np.stack([points * 0.0 + 1.0, points, 1.5 * points * points - 0.5])


def bspline(points):
    magnitude = np.abs(points)
    return np.where(
        magnitude <= 0.5,
        0.75 - magnitude * magnitude,
        np.where(magnitude <= 1.5, 0.5 * (1.5 - magnitude) ** 2, 0.0),
    )


def kernel_value(points):
    return 1.25 * bspline(points) - 0.125 * (bspline(points + 1.0) + bspline(points - 1.0))


def siac_table():
    nodes = np.array(GAUSS_NODES)
    weights = np.array(GAUSS_WEIGHTS)
    kernel_table = np.zeros((5, 3, 3))
    for slot_index in range(5):
        offset = slot_index - 2
        for low_end, high_end in ((-1.0, 0.0), (0.0, 1.0)):
            for node_value, node_weight in zip(GAUSS_NODES, GAUSS_WEIGHTS):
                xi_value = 0.5 * (low_end + high_end) + 0.5 * (high_end - low_end) * node_value
                outer_weight = 0.5 * (high_end - low_end) * node_weight
                breaks = [-1.0, 1.0]
                for spline_knot in (-2.5, -1.5, -0.5, 0.5, 1.5, 2.5):
                    crossing = xi_value - 2.0 * offset - 2.0 * spline_knot
                    if -1.0 < crossing < 1.0:
                        breaks.append(crossing)
                breaks = sorted(breaks)
                for piece_lo, piece_hi in zip(breaks[:-1], breaks[1:]):
                    eta_points = 0.5 * (piece_lo + piece_hi) + 0.5 * (piece_hi - piece_lo) * nodes
                    eta_weights = 0.5 * (piece_hi - piece_lo) * weights
                    samples = (
                        kernel_value(0.5 * xi_value - 0.5 * eta_points - offset) * eta_weights * 0.5
                    )
                    kernel_table[slot_index] += outer_weight * np.outer(
                        legendre_rows(np.array(xi_value)), legendre_rows(eta_points) @ samples
                    )
    return kernel_table * (np.arange(3)[None, :, None] + 0.5)


SUB = 8
LANE = 128
HALO = 3
GROUP = 2 * HALO
MODES = 9
FIELDS = 2 * MODES + 2
VEL_X = 2 * MODES
VEL_Y = 2 * MODES + 1
VMEM_BYTES = 40 * 1024 * 1024


def lanes_of(shape):
    return lax.broadcasted_iota(jnp.int32, shape, len(shape) - 1)


def rows_of(tile):
    return pl.ds(pl.multiple_of(tile * SUB, SUB), SUB)


def shift_rows(low, high, count):
    index = lax.broadcasted_iota(jnp.int32, low.shape, 0)
    return pltpu.roll(jnp.where(index < count, high, low), SUB - count, 0)


def roll_lanes(value, amount):
    width = value.shape[-1]
    return pltpu.roll(value, (-amount) % width, len(value.shape) - 1)


def upwind(speed, inner, outer):
    return jnp.maximum(speed, 0.0) * inner + jnp.minimum(speed, 0.0) * outer


def pack_tile(ext, pack, width, tile):
    rows = rows_of(tile)
    lane = lanes_of((SUB, LANE))
    packed = jnp.zeros((SUB, LANE), jnp.float32)
    for field in range(FIELDS):
        edges = jnp.where(
            lane < LANE // 2, ext[field, rows, 0:LANE], ext[field, rows, width - LANE : width]
        )
        moved = pltpu.roll(edges, (HALO + GROUP * field) % LANE, 1)
        inside = (lane >= GROUP * field) & (lane < GROUP * (field + 1))
        packed = jnp.where(inside, moved, packed)
    pack[rows, :] = packed


def unpack_tile(ext, from_west, from_east, width, tile):
    rows = rows_of(tile)
    lane = lanes_of((SUB, LANE))
    mixed = jnp.where(lax.rem(lane, GROUP) < HALO, from_west[rows, :], from_east[rows, :])
    for field in range(FIELDS):
        ext[field, rows, width : width + LANE] = pltpu.roll(
            mixed, (-(HALO + GROUP * field)) % LANE, 1
        )


def update_tile(ext, out, tiles, tile):
    here = rows_of(tile)
    below = rows_of(lax.rem(tile + (tiles - 1), tiles))
    above = rows_of(lax.rem(tile + 1, tiles))
    coeffs = [[ext[3 * i + j, here, :] for j in range(3)] for i in range(3)]
    vel_x = ext[VEL_X, here, :]
    vel_y = ext[VEL_Y, here, :]
    rate = [[None] * 3 for _ in range(3)]
    speed = 0.5 * (vel_x + roll_lanes(vel_x, 1))
    up, down = jnp.maximum(speed, 0.0), jnp.minimum(speed, 0.0)
    scale = STEP_SIZE * 2.0 / 3.0
    for j in range(3):
        even = coeffs[0][j] + coeffs[2][j]
        east_face = up * (even + coeffs[1][j]) + down * roll_lanes(even - coeffs[1][j], 1)
        west_face = roll_lanes(east_face, -1)
        change = east_face - west_face
        total = east_face + west_face
        rate[0][j] = (-0.5 * scale) * change
        rate[1][j] = (1.5 * scale) * (2.0 * vel_x * coeffs[0][j] - total)
        rate[2][j] = (2.5 * scale) * (2.0 * vel_x * coeffs[1][j] - change)
    speed_n = 0.5 * (vel_y + shift_rows(vel_y, ext[VEL_Y, above, :], 1))
    speed_s = 0.5 * (vel_y + shift_rows(ext[VEL_Y, below, :], vel_y, SUB - 1))
    up_n, down_n = jnp.maximum(speed_n, 0.0), jnp.minimum(speed_n, 0.0)
    up_s, down_s = jnp.maximum(speed_s, 0.0), jnp.minimum(speed_s, 0.0)
    for i in range(3):
        even = coeffs[i][0] + coeffs[i][2]
        north = even + coeffs[i][1]
        south = even - coeffs[i][1]
        south_above = ext[3 * i, above, :] - ext[3 * i + 1, above, :] + ext[3 * i + 2, above, :]
        north_below = ext[3 * i, below, :] + ext[3 * i + 1, below, :] + ext[3 * i + 2, below, :]
        north_face = up_n * north + down_n * shift_rows(south, south_above, 1)
        south_face = up_s * shift_rows(north_below, north, SUB - 1) + down_s * south
        change = north_face - south_face
        total = north_face + south_face
        along_y = (
            (-0.5 * scale) * change,
            (1.5 * scale) * (2.0 * vel_y * coeffs[i][0] - total),
            (2.5 * scale) * (2.0 * vel_y * coeffs[i][1] - change),
        )
        for j in range(3):
            mode = 3 * i + j
            out[mode, here, :] = (
                (1.0 / 3.0) * ext[MODES + mode, here, :]
                + (2.0 / 3.0) * coeffs[i][j]
                + (rate[i][j] + along_y[j])
            )


def advance_kernel(
    counts, start, section, vel_x, vel_y, out, ext, pack, from_west, from_east,
    load_sem, send_sem, recv_sem,
):
    height, width = vel_x.shape
    tiles = height // SUB + 1
    me_x, me_y = lax.axis_index("gx"), lax.axis_index("gy")

    def at(step_x, step_y):
        return {
            "gx": lax.rem(me_x + (step_x + counts[0]), counts[0]),
            "gy": lax.rem(me_y + (step_y + counts[1]), counts[1]),
        }

    inner = (pl.ds(0, height), pl.ds(0, width))
    sources = (
        (section, ext.at[(pl.ds(0, MODES),) + inner]),
        (start, ext.at[(pl.ds(MODES, MODES),) + inner]),
        (vel_x, ext.at[(VEL_X,) + inner]),
        (vel_y, ext.at[(VEL_Y,) + inner]),
    )
    loads = [
        pltpu.make_async_copy(source, target, load_sem.at[index])
        for index, (source, target) in enumerate(sources)
    ]
    for load in loads:
        load.start()

    around = [(i, j) for i in (-1, 0, 1) for j in (-1, 0, 1) if (i, j) != (0, 0)]
    barrier = pltpu.get_barrier_semaphore()
    for i, j in around:
        pl.semaphore_signal(
            barrier, inc=1, device_id=at(i, j), device_id_type=pl.DeviceIdType.MESH
        )
    pl.semaphore_wait(barrier, len(around))

    made = []

    def send(source, target, to):
        index = len(made)
        copy = pltpu.make_async_remote_copy(
            src_ref=source,
            dst_ref=target,
            send_sem=send_sem.at[index],
            recv_sem=recv_sem.at[index],
            device_id=to,
            device_id_type=pl.DeviceIdType.MESH,
        )
        copy.start()
        made.append(copy)

    low, high = pl.ds(0, HALO), pl.ds(height - HALO, HALO)
    north_halo, south_halo = pl.ds(height, HALO), pl.ds(height + SUB - HALO, HALO)
    wide = pl.ds(0, width)
    for rows, halo, step in ((low, north_halo, -1), (high, south_halo, 1)):
        send(section.at[:, rows, :], ext.at[pl.ds(0, MODES), halo, wide], at(0, step))
        send(start.at[:, rows, :], ext.at[pl.ds(MODES, MODES), halo, wide], at(0, step))
        send(vel_x.at[rows, :], ext.at[VEL_X, halo, wide], at(0, step))
        send(vel_y.at[rows, :], ext.at[VEL_Y, halo, wide], at(0, step))
    row_copies = list(made)

    for load in loads:
        load.wait()
    pl.loop(0, tiles - 1)(functools.partial(pack_tile, ext, pack, width))
    whole = pl.ds(0, height)
    send(pack.at[whole, :], from_west.at[whole, :], at(1, 0))
    send(pack.at[whole, :], from_east.at[whole, :], at(-1, 0))
    column_copies = made[len(row_copies) :]
    for rows, halo, step in ((low, north_halo, -1), (high, south_halo, 1)):
        send(pack.at[rows, :], from_west.at[halo, :], at(1, step))
        send(pack.at[rows, :], from_east.at[halo, :], at(-1, step))
    corner_copies = made[len(row_copies) + 2 :]

    for copy in column_copies:
        copy.wait_recv()
    pl.loop(0, tiles - 1)(functools.partial(unpack_tile, ext, from_west, from_east, width))
    pl.loop(1, tiles - 2)(functools.partial(update_tile, ext, out, tiles))
    for copy in row_copies + corner_copies:
        copy.wait_recv()
    unpack_tile(ext, from_west, from_east, width, tiles - 1)

    @pl.loop(tiles - 2, tiles + 1)
    def _(tile):
        update_tile(ext, out, tiles, lax.rem(tile, tiles))

    for copy in made:
        copy.wait_send()


def combine(table, middle, plus_1, minus_1, plus_2, minus_2):
    sums = []
    even_1 = [p + m for p, m in zip(plus_1, minus_1)]
    odd_1 = [p - m for p, m in zip(plus_1, minus_1)]
    even_2 = [p + m for p, m in zip(plus_2, minus_2)]
    odd_2 = [p - m for p, m in zip(plus_2, minus_2)]
    for to in range(3):
        total = None
        for degree in range(3):
            same = (to + degree) % 2 == 0
            terms = [
                (table[3][to][degree], (even_1 if same else odd_1)[degree]),
                (table[4][to][degree], (even_2 if same else odd_2)[degree]),
            ]
            if same:
                terms.append((table[2][to][degree], middle[degree]))
            for weight, value in terms:
                term = weight * value
                total = term if total is None else total + term
        sums.append(total)
    return sums


def filter_kernel(table, grid, updated, filtered, swept, result, copy_sem, out_sem):
    modes, height, width = updated.shape
    tiles = height // SUB + 1
    keep = pltpu.make_async_copy(
        grid.at[:, pl.ds(0, height), pl.ds(0, width)], updated, copy_sem
    )
    keep.start()

    @pl.loop(0, tiles)
    def _(tile):
        rows = rows_of(tile)
        for j in range(3):
            middle = [grid[3 * i + j, rows, :] for i in range(3)]
            moved = [[roll_lanes(m, k)[:, :width] for m in middle] for k in (1, -1, 2, -2)]
            sums = combine(table, [m[:, :width] for m in middle], *moved)
            for i in range(3):
                swept[3 * i + j, rows, :] = sums[i]

    @pl.loop(0, tiles - 1)
    def _(tile):
        here = rows_of(tile)
        below = rows_of(lax.rem(tile + (tiles - 1), tiles))
        above = rows_of(tile + 1)
        for i in range(3):
            middle = [swept[3 * i + j, here, :] for j in range(3)]
            high = [swept[3 * i + j, above, :] for j in range(3)]
            low = [swept[3 * i + j, below, :] for j in range(3)]
            sums = combine(
                table,
                middle,
                [shift_rows(m, h, 1) for m, h in zip(middle, high)],
                [shift_rows(l, m, SUB - 1) for m, l in zip(middle, low)],
                [shift_rows(m, h, 2) for m, h in zip(middle, high)],
                [shift_rows(l, m, SUB - 2) for m, l in zip(middle, low)],
            )
            for j in range(3):
                result[3 * i + j, here, :] = sums[j]
        pltpu.make_async_copy(
            result.at[:, here, :], filtered.at[:, here, :], out_sem.at[tile]
        ).start()

    @pl.loop(0, tiles - 1)
    def _(tile):
        here = rows_of(tile)
        pltpu.make_async_copy(
            result.at[:, here, :], filtered.at[:, here, :], out_sem.at[tile]
        ).wait()

    keep.wait()


def per_device(counts, start_coeffs, section_coeffs, vel_x, vel_y):
    modes, height, width = start_coeffs.shape
    tall, wide = height + SUB, width + LANE
    anywhere = pl.BlockSpec(memory_space=pl.ANY)
    local = pl.BlockSpec(memory_space=pltpu.VMEM)
    messages = 14
    grid = pl.pallas_call(
        functools.partial(advance_kernel, counts),
        out_shape=jax.ShapeDtypeStruct((modes, tall, wide), jnp.float32),
        in_specs=[anywhere] * 4,
        out_specs=local,
        scratch_shapes=[
            pltpu.VMEM((FIELDS, tall, wide), jnp.float32),
            pltpu.VMEM((height, LANE), jnp.float32),
            pltpu.VMEM((tall, LANE), jnp.float32),
            pltpu.VMEM((tall, LANE), jnp.float32),
            pltpu.SemaphoreType.DMA((4,)),
            pltpu.SemaphoreType.DMA((messages,)),
            pltpu.SemaphoreType.DMA((messages,)),
        ],
        compiler_params=pltpu.CompilerParams(
            collective_id=0, has_side_effects=True, vmem_limit_bytes=VMEM_BYTES
        ),
        name="advance",
    )(start_coeffs, section_coeffs, vel_x, vel_y)
    table = [[[float(v) for v in row] for row in part] for part in siac_table().astype(np.float32)]
    whole = jax.ShapeDtypeStruct((modes, height, width), jnp.float32)
    return pl.pallas_call(
        functools.partial(filter_kernel, table),
        out_shape=(whole, whole),
        in_specs=[local],
        out_specs=(anywhere, anywhere),
        scratch_shapes=[
            pltpu.VMEM((modes, tall, width), jnp.float32),
            pltpu.VMEM((modes, height, width), jnp.float32),
            pltpu.SemaphoreType.DMA,
            pltpu.SemaphoreType.DMA((height // SUB,)),
        ],
        compiler_params=pltpu.CompilerParams(vmem_limit_bytes=VMEM_BYTES),
        name="siac_filter",
    )(grid)


def solution(mesh):
    placed = (P(None, "gy", "gx"), P(None, "gy", "gx"), P("gy", "gx"), P("gy", "gx"))
    counts = (mesh.shape["gx"], mesh.shape["gy"])
    return jax.shard_map(
        functools.partial(per_device, counts),
        mesh=mesh,
        in_specs=placed,
        out_specs=(P(None, "gy", "gx"), P(None, "gy", "gx")),
        check_vma=False,
    )
```

```python
import functools

import jax
import jax.numpy as jnp
import numpy as np
from jax import lax
from jax.experimental import pallas as pl
from jax.experimental.pallas import tpu as pltpu
from jax.sharding import PartitionSpec as P

STEP_SIZE = 0.3
GAUSS_NODES = (
    -0.932469514203152,
    -0.6612093864662645,
    -0.2386191860831969,
    0.2386191860831969,
    0.6612093864662645,
    0.932469514203152,
)
GAUSS_WEIGHTS = (
    0.1713244923791704,
    0.3607615730481386,
    0.467913934572691,
    0.467913934572691,
    0.3607615730481386,
    0.1713244923791704,
)


def legendre_rows(points):
    return np.stack([points * 0.0 + 1.0, points, 1.5 * points * points - 0.5])


def bspline(points):
    magnitude = np.abs(points)
    return np.where(
        magnitude <= 0.5,
        0.75 - magnitude * magnitude,
        np.where(magnitude <= 1.5, 0.5 * (1.5 - magnitude) ** 2, 0.0),
    )


def kernel_value(points):
    return 1.25 * bspline(points) - 0.125 * (bspline(points + 1.0) + bspline(points - 1.0))


def siac_table():
    nodes = np.array(GAUSS_NODES)
    weights = np.array(GAUSS_WEIGHTS)
    kernel_table = np.zeros((5, 3, 3))
    for slot_index in range(5):
        offset = slot_index - 2
        for low_end, high_end in ((-1.0, 0.0), (0.0, 1.0)):
            for node_value, node_weight in zip(GAUSS_NODES, GAUSS_WEIGHTS):
                xi_value = 0.5 * (low_end + high_end) + 0.5 * (high_end - low_end) * node_value
                outer_weight = 0.5 * (high_end - low_end) * node_weight
                breaks = [-1.0, 1.0]
                for spline_knot in (-2.5, -1.5, -0.5, 0.5, 1.5, 2.5):
                    crossing = xi_value - 2.0 * offset - 2.0 * spline_knot
                    if -1.0 < crossing < 1.0:
                        breaks.append(crossing)
                breaks = sorted(breaks)
                for piece_lo, piece_hi in zip(breaks[:-1], breaks[1:]):
                    eta_points = 0.5 * (piece_lo + piece_hi) + 0.5 * (piece_hi - piece_lo) * nodes
                    eta_weights = 0.5 * (piece_hi - piece_lo) * weights
                    samples = (
                        kernel_value(0.5 * xi_value - 0.5 * eta_points - offset) * eta_weights * 0.5
                    )
                    kernel_table[slot_index] += outer_weight * np.outer(
                        legendre_rows(np.array(xi_value)), legendre_rows(eta_points) @ samples
                    )
    return kernel_table * (np.arange(3)[None, :, None] + 0.5)


SUB = 8
LANE = 128
HALO = 3
GROUP = 2 * HALO
MODES = 9
FIELDS = 2 * MODES + 2
VEL_X = 2 * MODES
VEL_Y = 2 * MODES + 1
VMEM_BYTES = 40 * 1024 * 1024


def lanes_of(shape):
    return lax.broadcasted_iota(jnp.int32, shape, len(shape) - 1)


def rows_of(tile):
    return pl.ds(pl.multiple_of(tile * SUB, SUB), SUB)


def shift_rows(low, high, count):
    index = lax.broadcasted_iota(jnp.int32, low.shape, 0)
    return pltpu.roll(jnp.where(index < count, high, low), SUB - count, 0)


def roll_lanes(value, amount):
    width = value.shape[-1]
    return pltpu.roll(value, (-amount) % width, len(value.shape) - 1)


def upwind(speed, inner, outer):
    return jnp.maximum(speed, 0.0) * inner + jnp.minimum(speed, 0.0) * outer


def pack_tile(ext, pack, width, tile):
    rows = rows_of(tile)
    lane = lanes_of((SUB, LANE))
    packed = jnp.zeros((SUB, LANE), jnp.float32)
    for field in range(FIELDS):
        edges = jnp.where(
            lane < LANE // 2, ext[field, rows, 0:LANE], ext[field, rows, width - LANE : width]
        )
        moved = pltpu.roll(edges, (HALO + GROUP * field) % LANE, 1)
        inside = (lane >= GROUP * field) & (lane < GROUP * (field + 1))
        packed = jnp.where(inside, moved, packed)
    pack[rows, :] = packed


def unpack_tile(ext, from_west, from_east, width, tile):
    rows = rows_of(tile)
    lane = lanes_of((SUB, LANE))
    mixed = jnp.where(lax.rem(lane, GROUP) < HALO, from_west[rows, :], from_east[rows, :])
    for field in range(FIELDS):
        ext[field, rows, width : width + LANE] = pltpu.roll(
            mixed, (-(HALO + GROUP * field)) % LANE, 1
        )


def update_tile(ext, out, tiles, tile):
    here = rows_of(tile)
    below = rows_of(lax.rem(tile + (tiles - 1), tiles))
    above = rows_of(lax.rem(tile + 1, tiles))
    coeffs = [[ext[3 * i + j, here, :] for j in range(3)] for i in range(3)]
    vel_x = ext[VEL_X, here, :]
    vel_y = ext[VEL_Y, here, :]
    rate = [[None] * 3 for _ in range(3)]
    speed = 0.5 * (vel_x + roll_lanes(vel_x, 1))
    up, down = jnp.maximum(speed, 0.0), jnp.minimum(speed, 0.0)
    scale = STEP_SIZE * 2.0 / 3.0
    for j in range(3):
        even = coeffs[0][j] + coeffs[2][j]
        east_face = up * (even + coeffs[1][j]) + down * roll_lanes(even - coeffs[1][j], 1)
        west_face = roll_lanes(east_face, -1)
        change = east_face - west_face
        total = east_face + west_face
        rate[0][j] = (-0.5 * scale) * change
        rate[1][j] = (1.5 * scale) * (2.0 * vel_x * coeffs[0][j] - total)
        rate[2][j] = (2.5 * scale) * (2.0 * vel_x * coeffs[1][j] - change)
    speed_n = 0.5 * (vel_y + shift_rows(vel_y, ext[VEL_Y, above, :], 1))
    speed_s = 0.5 * (vel_y + shift_rows(ext[VEL_Y, below, :], vel_y, SUB - 1))
    up_n, down_n = jnp.maximum(speed_n, 0.0), jnp.minimum(speed_n, 0.0)
    up_s, down_s = jnp.maximum(speed_s, 0.0), jnp.minimum(speed_s, 0.0)
    for i in range(3):
        even = coeffs[i][0] + coeffs[i][2]
        north = even + coeffs[i][1]
        south = even - coeffs[i][1]
        south_above = ext[3 * i, above, :] - ext[3 * i + 1, above, :] + ext[3 * i + 2, above, :]
        north_below = ext[3 * i, below, :] + ext[3 * i + 1, below, :] + ext[3 * i + 2, below, :]
        north_face = up_n * north + down_n * shift_rows(south, south_above, 1)
        south_face = up_s * shift_rows(north_below, north, SUB - 1) + down_s * south
        change = north_face - south_face
        total = north_face + south_face
        along_y = (
            (-0.5 * scale) * change,
            (1.5 * scale) * (2.0 * vel_y * coeffs[i][0] - total),
            (2.5 * scale) * (2.0 * vel_y * coeffs[i][1] - change),
        )
        for j in range(3):
            mode = 3 * i + j
            out[mode, here, :] = (
                (1.0 / 3.0) * ext[MODES + mode, here, :]
                + (2.0 / 3.0) * coeffs[i][j]
                + (rate[i][j] + along_y[j])
            )


def advance_kernel(
    counts, start, section, vel_x, vel_y, out, ext, pack, from_west, from_east,
    load_sem, send_sem, recv_sem,
):
    height, width = vel_x.shape
    tiles = height // SUB + 1
    me_x, me_y = lax.axis_index("gx"), lax.axis_index("gy")

    def at(step_x, step_y):
        return {
            "gx": lax.rem(me_x + (step_x + counts[0]), counts[0]),
            "gy": lax.rem(me_y + (step_y + counts[1]), counts[1]),
        }

    around = [(i, j) for i in (-1, 0, 1) for j in (-1, 0, 1) if (i, j) != (0, 0)]
    barrier = pltpu.get_barrier_semaphore()
    for i, j in around:
        pl.semaphore_signal(
            barrier, inc=1, device_id=at(i, j), device_id_type=pl.DeviceIdType.MESH
        )

    def load(columns, first_sem):
        inner = (pl.ds(0, height), columns)
        sources = (
            (section.at[:, :, columns], ext.at[(pl.ds(0, MODES),) + inner]),
            (start.at[:, :, columns], ext.at[(pl.ds(MODES, MODES),) + inner]),
            (vel_x.at[:, columns], ext.at[(VEL_X,) + inner]),
            (vel_y.at[:, columns], ext.at[(VEL_Y,) + inner]),
        )
        copies = [
            pltpu.make_async_copy(source, target, load_sem.at[first_sem + index])
            for index, (source, target) in enumerate(sources)
        ]
        for copy in copies:
            copy.start()
        return copies

    edge_loads = load(pl.ds(0, LANE), 0) + load(pl.ds(width - LANE, LANE), 4)
    inner_loads = load(pl.ds(LANE, width - 2 * LANE), 8)
    for copy in edge_loads:
        copy.wait()
    pl.loop(0, tiles - 1)(functools.partial(pack_tile, ext, pack, width))
    pl.semaphore_wait(barrier, len(around))

    made = []

    def send(source, target, to):
        index = len(made)
        copy = pltpu.make_async_remote_copy(
            src_ref=source,
            dst_ref=target,
            send_sem=send_sem.at[index],
            recv_sem=recv_sem.at[index],
            device_id=to,
            device_id_type=pl.DeviceIdType.MESH,
        )
        copy.start()
        made.append(copy)

    low, high = pl.ds(0, HALO), pl.ds(height - HALO, HALO)
    north_halo, south_halo = pl.ds(height, HALO), pl.ds(height + SUB - HALO, HALO)
    wide = pl.ds(0, width)
    whole = pl.ds(0, height)
    send(pack.at[whole, :], from_west.at[whole, :], at(1, 0))
    send(pack.at[whole, :], from_east.at[whole, :], at(-1, 0))
    column_copies = list(made)
    for rows, halo, step in ((low, north_halo, -1), (high, south_halo, 1)):
        send(pack.at[rows, :], from_west.at[halo, :], at(1, step))
        send(pack.at[rows, :], from_east.at[halo, :], at(-1, step))
    for rows, halo, step in ((low, north_halo, -1), (high, south_halo, 1)):
        send(section.at[:, rows, :], ext.at[pl.ds(0, MODES), halo, wide], at(0, step))
        send(start.at[:, rows, :], ext.at[pl.ds(MODES, MODES), halo, wide], at(0, step))
        send(vel_x.at[rows, :], ext.at[VEL_X, halo, wide], at(0, step))
        send(vel_y.at[rows, :], ext.at[VEL_Y, halo, wide], at(0, step))
    row_copies = made[len(column_copies) :]

    for copy in inner_loads:
        copy.wait()
    for copy in column_copies:
        copy.wait_recv()
    pl.loop(0, tiles - 1)(functools.partial(unpack_tile, ext, from_west, from_east, width))
    pl.loop(1, tiles - 2)(functools.partial(update_tile, ext, out, tiles))
    for copy in row_copies:
        copy.wait_recv()
    unpack_tile(ext, from_west, from_east, width, tiles - 1)

    @pl.loop(tiles - 2, tiles + 1)
    def _(tile):
        update_tile(ext, out, tiles, lax.rem(tile, tiles))

    for copy in made:
        copy.wait_send()


def combine(table, middle, plus_1, minus_1, plus_2, minus_2):
    sums = []
    even_1 = [p + m for p, m in zip(plus_1, minus_1)]
    odd_1 = [p - m for p, m in zip(plus_1, minus_1)]
    even_2 = [p + m for p, m in zip(plus_2, minus_2)]
    odd_2 = [p - m for p, m in zip(plus_2, minus_2)]
    for to in range(3):
        total = None
        for degree in range(3):
            same = (to + degree) % 2 == 0
            terms = [
                (table[3][to][degree], (even_1 if same else odd_1)[degree]),
                (table[4][to][degree], (even_2 if same else odd_2)[degree]),
            ]
            if same:
                terms.append((table[2][to][degree], middle[degree]))
            for weight, value in terms:
                term = weight * value
                total = term if total is None else total + term
        sums.append(total)
    return sums


def filter_kernel(table, grid, updated, filtered, swept, result, copy_sem, out_sem):
    modes, height, width = updated.shape
    tiles = height // SUB + 1
    keep = pltpu.make_async_copy(
        grid.at[:, pl.ds(0, height), pl.ds(0, width)], updated, copy_sem
    )
    keep.start()

    @pl.loop(0, tiles)
    def _(tile):
        rows = rows_of(tile)
        for j in range(3):
            middle = [grid[3 * i + j, rows, :] for i in range(3)]
            moved = [[roll_lanes(m, k)[:, :width] for m in middle] for k in (1, -1, 2, -2)]
            sums = combine(table, [m[:, :width] for m in middle], *moved)
            for i in range(3):
                swept[3 * i + j, rows, :] = sums[i]

    @pl.loop(0, tiles - 1)
    def _(tile):
        here = rows_of(tile)
        below = rows_of(lax.rem(tile + (tiles - 1), tiles))
        above = rows_of(tile + 1)
        for i in range(3):
            middle = [swept[3 * i + j, here, :] for j in range(3)]
            high = [swept[3 * i + j, above, :] for j in range(3)]
            low = [swept[3 * i + j, below, :] for j in range(3)]
            sums = combine(
                table,
                middle,
                [shift_rows(m, h, 1) for m, h in zip(middle, high)],
                [shift_rows(l, m, SUB - 1) for m, l in zip(middle, low)],
                [shift_rows(m, h, 2) for m, h in zip(middle, high)],
                [shift_rows(l, m, SUB - 2) for m, l in zip(middle, low)],
            )
            for j in range(3):
                result[3 * i + j, here, :] = sums[j]
        pltpu.make_async_copy(
            result.at[:, here, :], filtered.at[:, here, :], out_sem.at[tile]
        ).start()

    @pl.loop(0, tiles - 1)
    def _(tile):
        here = rows_of(tile)
        pltpu.make_async_copy(
            result.at[:, here, :], filtered.at[:, here, :], out_sem.at[tile]
        ).wait()

    keep.wait()


def per_device(counts, start_coeffs, section_coeffs, vel_x, vel_y):
    modes, height, width = start_coeffs.shape
    tall, wide = height + SUB, width + LANE
    anywhere = pl.BlockSpec(memory_space=pltpu.HBM)
    local = pl.BlockSpec(memory_space=pltpu.VMEM)
    messages = 14
    inputs = [
        pltpu.with_memory_space_constraint(value, pltpu.HBM)
        for value in (start_coeffs, section_coeffs, vel_x, vel_y)
    ]
    grid = pl.pallas_call(
        functools.partial(advance_kernel, counts),
        out_shape=jax.ShapeDtypeStruct((modes, tall, wide), jnp.float32),
        in_specs=[anywhere] * 4,
        out_specs=local,
        scratch_shapes=[
            pltpu.VMEM((FIELDS, tall, wide), jnp.float32),
            pltpu.VMEM((height, LANE), jnp.float32),
            pltpu.VMEM((tall, LANE), jnp.float32),
            pltpu.VMEM((tall, LANE), jnp.float32),
            pltpu.SemaphoreType.DMA((12,)),
            pltpu.SemaphoreType.DMA((messages,)),
            pltpu.SemaphoreType.DMA((messages,)),
        ],
        compiler_params=pltpu.CompilerParams(
            collective_id=0, has_side_effects=True, vmem_limit_bytes=VMEM_BYTES
        ),
        name="advance",
    )(*inputs)
    table = [[[float(v) for v in row] for row in part] for part in siac_table().astype(np.float32)]
    whole = jax.ShapeDtypeStruct((modes, height, width), jnp.float32)
    return pl.pallas_call(
        functools.partial(filter_kernel, table),
        out_shape=(whole, whole),
        in_specs=[local],
        out_specs=(anywhere, anywhere),
        scratch_shapes=[
            pltpu.VMEM((modes, tall, width), jnp.float32),
            pltpu.VMEM((modes, height, width), jnp.float32),
            pltpu.SemaphoreType.DMA,
            pltpu.SemaphoreType.DMA((height // SUB,)),
        ],
        compiler_params=pltpu.CompilerParams(vmem_limit_bytes=VMEM_BYTES),
        name="siac_filter",
    )(grid)


def solution(mesh):
    placed = (P(None, "gy", "gx"), P(None, "gy", "gx"), P("gy", "gx"), P("gy", "gx"))
    counts = (mesh.shape["gx"], mesh.shape["gy"])
    return jax.shard_map(
        functools.partial(per_device, counts),
        mesh=mesh,
        in_specs=placed,
        out_specs=(P(None, "gy", "gx"), P(None, "gy", "gx")),
        check_vma=False,
    )
```

```python
import functools

import jax
import jax.numpy as jnp
import numpy as np
from jax import lax
from jax.experimental import pallas as pl
from jax.experimental.pallas import tpu as pltpu
from jax.sharding import PartitionSpec as P

STEP_SIZE = 0.3
GAUSS_NODES = (
    -0.932469514203152,
    -0.6612093864662645,
    -0.2386191860831969,
    0.2386191860831969,
    0.6612093864662645,
    0.932469514203152,
)
GAUSS_WEIGHTS = (
    0.1713244923791704,
    0.3607615730481386,
    0.467913934572691,
    0.467913934572691,
    0.3607615730481386,
    0.1713244923791704,
)


def legendre_rows(points):
    return np.stack([points * 0.0 + 1.0, points, 1.5 * points * points - 0.5])


def bspline(points):
    magnitude = np.abs(points)
    return np.where(
        magnitude <= 0.5,
        0.75 - magnitude * magnitude,
        np.where(magnitude <= 1.5, 0.5 * (1.5 - magnitude) ** 2, 0.0),
    )


def kernel_value(points):
    return 1.25 * bspline(points) - 0.125 * (bspline(points + 1.0) + bspline(points - 1.0))


def siac_table():
    nodes = np.array(GAUSS_NODES)
    weights = np.array(GAUSS_WEIGHTS)
    kernel_table = np.zeros((5, 3, 3))
    for slot_index in range(5):
        offset = slot_index - 2
        for low_end, high_end in ((-1.0, 0.0), (0.0, 1.0)):
            for node_value, node_weight in zip(GAUSS_NODES, GAUSS_WEIGHTS):
                xi_value = 0.5 * (low_end + high_end) + 0.5 * (high_end - low_end) * node_value
                outer_weight = 0.5 * (high_end - low_end) * node_weight
                breaks = [-1.0, 1.0]
                for spline_knot in (-2.5, -1.5, -0.5, 0.5, 1.5, 2.5):
                    crossing = xi_value - 2.0 * offset - 2.0 * spline_knot
                    if -1.0 < crossing < 1.0:
                        breaks.append(crossing)
                breaks = sorted(breaks)
                for piece_lo, piece_hi in zip(breaks[:-1], breaks[1:]):
                    eta_points = 0.5 * (piece_lo + piece_hi) + 0.5 * (piece_hi - piece_lo) * nodes
                    eta_weights = 0.5 * (piece_hi - piece_lo) * weights
                    samples = (
                        kernel_value(0.5 * xi_value - 0.5 * eta_points - offset) * eta_weights * 0.5
                    )
                    kernel_table[slot_index] += outer_weight * np.outer(
                        legendre_rows(np.array(xi_value)), legendre_rows(eta_points) @ samples
                    )
    return kernel_table * (np.arange(3)[None, :, None] + 0.5)


SUB = 8
LANE = 128
HALO = 3
GROUP = 2 * HALO
MODES = 9
FIELDS = 2 * MODES + 2
VEL_X = 2 * MODES
VEL_Y = 2 * MODES + 1
UNROLL = 7
VMEM_BYTES = 40 * 1024 * 1024


def lanes_of(shape):
    return lax.broadcasted_iota(jnp.int32, shape, len(shape) - 1)


def rows_of(tile):
    return pl.ds(pl.multiple_of(tile * SUB, SUB), SUB)


def shift_rows(low, high, count):
    index = lax.broadcasted_iota(jnp.int32, low.shape, 0)
    return pltpu.roll(jnp.where(index < count, high, low), SUB - count, 0)


def roll_lanes(value, amount):
    width = value.shape[-1]
    return pltpu.roll(value, (-amount) % width, len(value.shape) - 1)


def upwind(speed, inner, outer):
    return jnp.maximum(speed, 0.0) * inner + jnp.minimum(speed, 0.0) * outer


def pack_tile(ext, pack, width, tile):
    rows = rows_of(tile)
    lane = lanes_of((SUB, LANE))
    packed = jnp.zeros((SUB, LANE), jnp.float32)
    for field in range(FIELDS):
        edges = jnp.where(
            lane < LANE // 2, ext[field, rows, 0:LANE], ext[field, rows, width - LANE : width]
        )
        moved = pltpu.roll(edges, (HALO + GROUP * field) % LANE, 1)
        inside = (lane >= GROUP * field) & (lane < GROUP * (field + 1))
        packed = jnp.where(inside, moved, packed)
    pack[rows, :] = packed


def unpack_tile(ext, from_west, from_east, width, tile):
    rows = rows_of(tile)
    lane = lanes_of((SUB, LANE))
    mixed = jnp.where(lax.rem(lane, GROUP) < HALO, from_west[rows, :], from_east[rows, :])
    for field in range(FIELDS):
        ext[field, rows, width : width + LANE] = pltpu.roll(
            mixed, (-(HALO + GROUP * field)) % LANE, 1
        )


def update_tile(ext, out, tiles, tile):
    here = rows_of(tile)
    below = rows_of(lax.rem(tile + (tiles - 1), tiles))
    above = rows_of(lax.rem(tile + 1, tiles))
    coeffs = [[ext[3 * i + j, here, :] for j in range(3)] for i in range(3)]
    vel_x = ext[VEL_X, here, :]
    vel_y = ext[VEL_Y, here, :]
    rate = [[None] * 3 for _ in range(3)]
    speed = 0.5 * (vel_x + roll_lanes(vel_x, 1))
    up, down = jnp.maximum(speed, 0.0), jnp.minimum(speed, 0.0)
    scale = STEP_SIZE * 2.0 / 3.0
    for j in range(3):
        even = coeffs[0][j] + coeffs[2][j]
        east_face = up * (even + coeffs[1][j]) + down * roll_lanes(even - coeffs[1][j], 1)
        west_face = roll_lanes(east_face, -1)
        change = east_face - west_face
        total = east_face + west_face
        rate[0][j] = (-0.5 * scale) * change
        rate[1][j] = (1.5 * scale) * (2.0 * vel_x * coeffs[0][j] - total)
        rate[2][j] = (2.5 * scale) * (2.0 * vel_x * coeffs[1][j] - change)
    speed_n = 0.5 * (vel_y + shift_rows(vel_y, ext[VEL_Y, above, :], 1))
    speed_s = 0.5 * (vel_y + shift_rows(ext[VEL_Y, below, :], vel_y, SUB - 1))
    up_n, down_n = jnp.maximum(speed_n, 0.0), jnp.minimum(speed_n, 0.0)
    up_s, down_s = jnp.maximum(speed_s, 0.0), jnp.minimum(speed_s, 0.0)
    for i in range(3):
        even = coeffs[i][0] + coeffs[i][2]
        north = even + coeffs[i][1]
        south = even - coeffs[i][1]
        south_above = ext[3 * i, above, :] - ext[3 * i + 1, above, :] + ext[3 * i + 2, above, :]
        north_below = ext[3 * i, below, :] + ext[3 * i + 1, below, :] + ext[3 * i + 2, below, :]
        north_face = up_n * north + down_n * shift_rows(south, south_above, 1)
        south_face = up_s * shift_rows(north_below, north, SUB - 1) + down_s * south
        change = north_face - south_face
        total = north_face + south_face
        along_y = (
            (-0.5 * scale) * change,
            (1.5 * scale) * (2.0 * vel_y * coeffs[i][0] - total),
            (2.5 * scale) * (2.0 * vel_y * coeffs[i][1] - change),
        )
        for j in range(3):
            mode = 3 * i + j
            out[mode, here, :] = (
                (1.0 / 3.0) * ext[MODES + mode, here, :]
                + (2.0 / 3.0) * coeffs[i][j]
                + (rate[i][j] + along_y[j])
            )


def advance_kernel(
    counts, start, section, vel_x, vel_y, out, ext, pack, from_west, from_east,
    load_sem, send_sem, recv_sem,
):
    height, width = vel_x.shape
    tiles = height // SUB + 1
    me_x, me_y = lax.axis_index("gx"), lax.axis_index("gy")

    def at(step_x, step_y):
        return {
            "gx": lax.rem(me_x + (step_x + counts[0]), counts[0]),
            "gy": lax.rem(me_y + (step_y + counts[1]), counts[1]),
        }

    around = [(i, j) for i in (-1, 0, 1) for j in (-1, 0, 1) if (i, j) != (0, 0)]
    barrier = pltpu.get_barrier_semaphore()
    for i, j in around:
        pl.semaphore_signal(
            barrier, inc=1, device_id=at(i, j), device_id_type=pl.DeviceIdType.MESH
        )

    def load(columns, first_sem):
        inner = (pl.ds(0, height), columns)
        sources = (
            (section.at[:, :, columns], ext.at[(pl.ds(0, MODES),) + inner]),
            (start.at[:, :, columns], ext.at[(pl.ds(MODES, MODES),) + inner]),
            (vel_x.at[:, columns], ext.at[(VEL_X,) + inner]),
            (vel_y.at[:, columns], ext.at[(VEL_Y,) + inner]),
        )
        copies = [
            pltpu.make_async_copy(source, target, load_sem.at[first_sem + index])
            for index, (source, target) in enumerate(sources)
        ]
        for copy in copies:
            copy.start()
        return copies

    edge_loads = load(pl.ds(0, LANE), 0) + load(pl.ds(width - LANE, LANE), 4)
    inner_loads = load(pl.ds(LANE, width - 2 * LANE), 8)
    for copy in edge_loads:
        copy.wait()
    pl.loop(0, tiles - 1, unroll=8)(functools.partial(pack_tile, ext, pack, width))
    pl.semaphore_wait(barrier, len(around))

    made = []

    def send(source, target, to):
        index = len(made)
        copy = pltpu.make_async_remote_copy(
            src_ref=source,
            dst_ref=target,
            send_sem=send_sem.at[index],
            recv_sem=recv_sem.at[index],
            device_id=to,
            device_id_type=pl.DeviceIdType.MESH,
        )
        copy.start()
        made.append(copy)

    low, high = pl.ds(0, HALO), pl.ds(height - HALO, HALO)
    north_halo, south_halo = pl.ds(height, HALO), pl.ds(height + SUB - HALO, HALO)
    wide = pl.ds(0, width)
    whole = pl.ds(0, height)
    send(pack.at[whole, :], from_west.at[whole, :], at(1, 0))
    send(pack.at[whole, :], from_east.at[whole, :], at(-1, 0))
    column_copies = list(made)
    for rows, halo, step in ((low, north_halo, -1), (high, south_halo, 1)):
        send(pack.at[rows, :], from_west.at[halo, :], at(1, step))
        send(pack.at[rows, :], from_east.at[halo, :], at(-1, step))
    for rows, halo, step in ((low, north_halo, -1), (high, south_halo, 1)):
        send(section.at[:, rows, :], ext.at[pl.ds(0, MODES), halo, wide], at(0, step))
        send(start.at[:, rows, :], ext.at[pl.ds(MODES, MODES), halo, wide], at(0, step))
        send(vel_x.at[rows, :], ext.at[VEL_X, halo, wide], at(0, step))
        send(vel_y.at[rows, :], ext.at[VEL_Y, halo, wide], at(0, step))
    row_copies = made[len(column_copies) :]

    for copy in inner_loads:
        copy.wait()
    for copy in column_copies:
        copy.wait_recv()
    pl.loop(0, tiles - 1, unroll=8)(functools.partial(unpack_tile, ext, from_west, from_east, width))
    pl.loop(1, tiles - 2, unroll=6)(functools.partial(update_tile, ext, out, tiles))
    for copy in row_copies:
        copy.wait_recv()
    unpack_tile(ext, from_west, from_east, width, tiles - 1)

    @pl.loop(tiles - 2, tiles + 1, unroll=3)
    def _(tile):
        update_tile(ext, out, tiles, lax.rem(tile, tiles))

    for copy in made:
        copy.wait_send()


def combine(table, middle, plus_1, minus_1, plus_2, minus_2):
    sums = []
    even_1 = [p + m for p, m in zip(plus_1, minus_1)]
    odd_1 = [p - m for p, m in zip(plus_1, minus_1)]
    even_2 = [p + m for p, m in zip(plus_2, minus_2)]
    odd_2 = [p - m for p, m in zip(plus_2, minus_2)]
    for to in range(3):
        total = None
        for degree in range(3):
            same = (to + degree) % 2 == 0
            terms = [
                (table[3][to][degree], (even_1 if same else odd_1)[degree]),
                (table[4][to][degree], (even_2 if same else odd_2)[degree]),
            ]
            if same:
                terms.append((table[2][to][degree], middle[degree]))
            for weight, value in terms:
                term = weight * value
                total = term if total is None else total + term
        sums.append(total)
    return sums


def filter_kernel(table, grid, updated, filtered, swept, result, copy_sem, out_sem):
    modes, height, width = updated.shape
    tiles = height // SUB + 1
    keep = pltpu.make_async_copy(
        grid.at[:, pl.ds(0, height), pl.ds(0, width)], updated, copy_sem
    )
    keep.start()

    def sweep_x(tile):
        rows = rows_of(tile)
        for j in range(3):
            middle = [grid[3 * i + j, rows, :] for i in range(3)]
            moved = [[roll_lanes(m, k)[:, :width] for m in middle] for k in (1, -1, 2, -2)]
            sums = combine(table, [m[:, :width] for m in middle], *moved)
            for i in range(3):
                swept[3 * i + j, rows, :] = sums[i]

    def sweep_y(tile):
        here = rows_of(tile)
        below = rows_of(lax.rem(tile + (tiles - 1), tiles))
        above = rows_of(tile + 1)
        for i in range(3):
            middle = [swept[3 * i + j, here, :] for j in range(3)]
            high = [swept[3 * i + j, above, :] for j in range(3)]
            low = [swept[3 * i + j, below, :] for j in range(3)]
            sums = combine(
                table,
                middle,
                [shift_rows(m, h, 1) for m, h in zip(middle, high)],
                [shift_rows(l, m, SUB - 1) for m, l in zip(middle, low)],
                [shift_rows(m, h, 2) for m, h in zip(middle, high)],
                [shift_rows(l, m, SUB - 2) for m, l in zip(middle, low)],
            )
            for j in range(3):
                result[3 * i + j, here, :] = sums[j]
        pltpu.make_async_copy(
            result.at[:, here, :], filtered.at[:, here, :], out_sem.at[tile]
        ).start()

    sweep_x(tiles - 1)
    sweep_x(0)

    @pl.loop(0, tiles - 2, unroll=UNROLL)
    def _(tile):
        sweep_x(tile + 1)
        sweep_y(tile)

    sweep_y(tiles - 2)

    @pl.loop(0, tiles - 1)
    def _(tile):
        here = rows_of(tile)
        pltpu.make_async_copy(
            result.at[:, here, :], filtered.at[:, here, :], out_sem.at[tile]
        ).wait()

    keep.wait()


def per_device(counts, start_coeffs, section_coeffs, vel_x, vel_y):
    modes, height, width = start_coeffs.shape
    tall, wide = height + SUB, width + LANE
    anywhere = pl.BlockSpec(memory_space=pltpu.HBM)
    local = pl.BlockSpec(memory_space=pltpu.VMEM)
    messages = 14
    inputs = [
        pltpu.with_memory_space_constraint(value, pltpu.HBM)
        for value in (start_coeffs, section_coeffs, vel_x, vel_y)
    ]
    grid = pl.pallas_call(
        functools.partial(advance_kernel, counts),
        out_shape=jax.ShapeDtypeStruct((modes, tall, wide), jnp.float32),
        in_specs=[anywhere] * 4,
        out_specs=local,
        scratch_shapes=[
            pltpu.VMEM((FIELDS, tall, wide), jnp.float32),
            pltpu.VMEM((height, LANE), jnp.float32),
            pltpu.VMEM((tall, LANE), jnp.float32),
            pltpu.VMEM((tall, LANE), jnp.float32),
            pltpu.SemaphoreType.DMA((12,)),
            pltpu.SemaphoreType.DMA((messages,)),
            pltpu.SemaphoreType.DMA((messages,)),
        ],
        compiler_params=pltpu.CompilerParams(
            collective_id=0, has_side_effects=True, vmem_limit_bytes=VMEM_BYTES
        ),
        name="advance",
    )(*inputs)
    table = [[[float(v) for v in row] for row in part] for part in siac_table().astype(np.float32)]
    whole = jax.ShapeDtypeStruct((modes, height, width), jnp.float32)
    return pl.pallas_call(
        functools.partial(filter_kernel, table),
        out_shape=(whole, whole),
        in_specs=[local],
        out_specs=(anywhere, anywhere),
        scratch_shapes=[
            pltpu.VMEM((modes, tall, width), jnp.float32),
            pltpu.VMEM((modes, height, width), jnp.float32),
            pltpu.SemaphoreType.DMA,
            pltpu.SemaphoreType.DMA((height // SUB,)),
        ],
        compiler_params=pltpu.CompilerParams(vmem_limit_bytes=VMEM_BYTES),
        name="siac_filter",
    )(grid)


def solution(mesh):
    placed = (P(None, "gy", "gx"), P(None, "gy", "gx"), P("gy", "gx"), P("gy", "gx"))
    counts = (mesh.shape["gx"], mesh.shape["gy"])
    return jax.shard_map(
        functools.partial(per_device, counts),
        mesh=mesh,
        in_specs=placed,
        out_specs=(P(None, "gy", "gx"), P(None, "gy", "gx")),
        check_vma=False,
    )
```
